32 devices in a mesh: row: 8 (over z, core), col: 4 (over y, x).
Axes of the slice: x: 2, y: 2, z: 4, core: 2. Of those that a mesh axis runs over, the one named last changes fastest.
Arguments:
- object_field: float32 [2, 2048, 1024], P(None, 'row', 'col'), may hold values from -1.8 to 1.8
- probe: float32 [2, 256, 256], replicated, may hold values from -0.4 to 0.4
- coeffs: float32 [3, 256, 256], replicated, may hold values from 0.5 to 1.5
- patterns: float32 [8, 4, 4, 256, 256], P('row', 'col'), may hold values from 0 to 1
- offsets: int32 [8, 4, 4, 2], P('row', 'col'), may hold values from 0 to 255
Outputs:
- object_out: float32 [2, 2048, 1024], P(None, 'row', 'col')
- coeffs_out: float32 [3, 256, 256], replicated
The draws below stay inside these ranges and needn't reach their ends.
All inputs are finite; a program needn't handle non-finite values.
Results may differ from the reference program's by a relative error of at most 0.0003.
Values sent between devices are 32-bit elements; how exact they have to be, the bound alone decides.
A program may use at most 64 MiB of HBM per device.

```python
import jax
import jax.numpy as jnp
from jax import lax

WIN = 256
TILE = 256
POS = 4
ITERS = 2
NY = 2048
NX = 1024
N_ROW = 8
N_COL = 4


def phased_field(key, rows, cols, low, high):
    amp_key, phase_key = jax.random.split(key)
    amplitude = jax.random.uniform(amp_key, (rows, cols), jnp.float32, low, high)
    phase = jax.random.uniform(phase_key, (rows, cols), jnp.float32, -jnp.pi, jnp.pi)
    return jnp.stack([amplitude * jnp.cos(phase), amplitude * jnp.sin(phase)])


def draw_object_field(key, part):
    folded = jax.random.fold_in(key, 11)
    return phased_field(folded, NY, NX, 0.5, 1.5)


def draw_probe(key, part):
    folded = jax.random.fold_in(key, 23)
    return phased_field(folded, WIN, WIN, 0.15, 0.35)


def set_ends(entries, stream_key, least, largest):
    longest = entries.shape.index(max(entries.shape))
    spots = []
    for shift in (0, 1):
        where = [jax.random.randint(jax.random.fold_in(stream_key, axis), (), 0, length) for axis, length in enumerate(entries.shape)]
        where[longest] = (where[longest] + shift) % entries.shape[longest]
        spots.append(tuple(where))
    return entries.at[spots[0]].set(least).at[spots[1]].set(largest)


def level_of(stream_key, shape, cuts, least, largest):
    level = 1.0
    for axis_at, blocks in cuts:
        steps = jax.random.uniform(jax.random.fold_in(jax.random.fold_in(stream_key, 6), axis_at), (blocks,), jnp.float32, least / len(cuts), largest / len(cuts))
        level = level * jnp.repeat(jnp.exp(steps), shape[axis_at] // blocks).reshape((-1,) + (1,) * (len(shape) - 1 - axis_at))
    return level


def setup_inputs(seed: int = 0) -> dict:
    streams_of = jax.random.split(jax.random.key(seed), 6)
    object_field = draw_object_field(jax.random.fold_in(streams_of[5], 71), 0)
    probe = draw_probe(jax.random.fold_in(streams_of[5], 71), 0)
    coeffs = jnp.clip(jax.random.uniform(streams_of[2], (3, WIN, WIN), jnp.float32, 0.5, 1.5), 0.5, 1.5)
    patterns = jnp.clip(1.0 * jax.random.uniform(streams_of[3], (N_ROW, N_COL, POS, WIN, WIN), jnp.float32) ** level_of(streams_of[3], (N_ROW, N_COL, POS, WIN, WIN), ((0, 8), (1, 4)), -0.2, 0.2), 0.0, 1.0)
    offsets = set_ends(jax.random.randint(streams_of[4], (N_ROW, N_COL, POS, 2), 0, TILE), jax.random.fold_in(streams_of[4], 1), 0, TILE - 1).astype(jnp.int32)
    return dict(object_field=object_field, probe=probe, coeffs=coeffs, patterns=patterns, offsets=offsets)


STEP_RATE = 0.2
RIDGE = 1.0
EPSILON = 1e-06

def dft_parts(order):
    index = jnp.arange(order, dtype=jnp.int32)
    product = index[:, None] * index[None, :] % order
    angle = -2.0 * jnp.pi / order * product.astype(jnp.float32)
    factor = 1.0 / jnp.sqrt(jnp.float32(order))
    return (jnp.cos(angle) * factor, jnp.sin(angle) * factor)

def matmul(left, right):
    return jnp.dot(left, right, precision=lax.Precision.HIGHEST, preferred_element_type=jnp.float32)

def transform(real, imag, mat_real, mat_imag):
    first_real = matmul(mat_real, real) - matmul(mat_imag, imag)
    first_imag = matmul(mat_real, imag) + matmul(mat_imag, real)
    second_real = matmul(first_real, mat_real) - matmul(first_imag, mat_imag)
    second_imag = matmul(first_real, mat_imag) + matmul(first_imag, mat_real)
    return (second_real, second_imag)

def window_step(window, probe, coeffs, pattern, mat_real, mat_imag):
    probe_real, probe_imag = (probe[0], probe[1])
    exit_real = probe_real * window[0] - probe_imag * window[1]
    exit_imag = probe_real * window[1] + probe_imag * window[0]
    wave_real, wave_imag = transform(exit_real, exit_imag, mat_real, mat_imag)
    inten = wave_real * wave_real + wave_imag * wave_imag
    lin, quad, cubic = (coeffs[0], coeffs[1], coeffs[2])
    response = inten * (lin + inten * (quad + inten * cubic))
    error = response - pattern
    slope = lin + inten * (2.0 * quad + 3.0 * cubic * inten)
    weight = 2.0 * error * slope
    back_real, back_imag = transform(weight * wave_real, weight * wave_imag, mat_real, -mat_imag)
    grad_real = probe_real * back_real + probe_imag * back_imag
    grad_imag = probe_real * back_imag - probe_imag * back_real
    squared = inten * inten
    gsums = jnp.stack([error * inten, error * squared, error * squared * inten])
    hsums = jnp.stack([squared, squared * squared, squared * squared * squared])
    return (jnp.stack([grad_real, grad_imag]), gsums, hsums)

def reference(object_field, probe, coeffs, patterns, offsets):
    mat_real, mat_imag = dft_parts(WIN)
    half = WIN // 2
    rows_all = object_field.shape[1]
    cols_all = object_field.shape[2]
    count = N_ROW * N_COL * POS
    flat_pats = patterns.reshape(count, WIN, WIN)
    flat_offs = offsets.reshape(count, 2)
    index = jnp.arange(count, dtype=jnp.int32)
    start_rows = index // (N_COL * POS) * TILE + flat_offs[:, 0]
    start_cols = index // POS % N_COL * TILE + flat_offs[:, 1]
    zero = jnp.zeros((), jnp.int32)
    total = 2.0 * rows_all * cols_all
    for turn in range(ITERS):
        padded = jnp.pad(object_field, ((0, 0), (half, half), (half, half)))

        def visit(carry, item):
            grad_pad, gsums, hsums = carry
            row_start, col_start, pattern = item
            window = lax.dynamic_slice(padded, (zero, row_start, col_start), (2, WIN, WIN))
            grad_win, gterm, hterm = window_step(window, probe, coeffs, pattern, mat_real, mat_imag)
            current = lax.dynamic_slice(grad_pad, (zero, row_start, col_start), (2, WIN, WIN))
            grad_pad = lax.dynamic_update_slice(grad_pad, current + grad_win, (zero, row_start, col_start))
            return ((grad_pad, gsums + gterm, hsums + hterm), None)
        start = (jnp.zeros_like(padded), jnp.zeros((3, WIN, WIN), jnp.float32), jnp.zeros((3, WIN, WIN), jnp.float32))
        (grad_pad, gsums, hsums), _ = lax.scan(visit, start, (start_rows, start_cols, flat_pats))
        grad = grad_pad[:, half:half + rows_all, half:half + cols_all]
        meansq = jnp.sum(grad * grad) / total
        coeffs = coeffs - gsums / (hsums + RIDGE)
        object_field = object_field - STEP_RATE * grad / jnp.sqrt(meansq + EPSILON)
    return (object_field, coeffs)
```

```python
import functools

import jax
import jax.numpy as jnp
import ml_dtypes
import numpy as np
from jax import lax
from jax.experimental import pallas as pl
from jax.experimental.pallas import tpu as pltpu
from jax.sharding import PartitionSpec as P

ITERS = 2


STEP_RATE = 0.2
RIDGE = 1.0
EPSILON = 1e-06


def passed_along(block, axis, distance):
    devices = range(lax.axis_size(axis))
    route = [(i - distance, i) for i in devices if i - distance in devices]
    return lax.ppermute(block, axis, route)


def padded(block, sides, width):
    for axis, dim in sides:
        count = lax.axis_size(axis)
        forward = [(i, i + 1) for i in range(count - 1)]
        backward = [(target, source) for source, target in forward]
        low = lax.ppermute(
            lax.slice_in_dim(block, block.shape[dim] - width, None, axis=dim), axis, forward
        )
        high = lax.ppermute(lax.slice_in_dim(block, 0, width, axis=dim), axis, backward)
        block = jnp.concatenate([low, block, high], axis=dim)
    return block


def dft_stacks(order):
    index = np.arange(order)
    angle = -2.0 * np.pi / order * (index[:, None] * index[None, :] % order)
    real, imag = np.cos(angle) / np.sqrt(order), np.sin(angle) / np.sqrt(order)
    left = np.block([[real, -imag], [imag, real]]).astype(np.float32)
    stacks = []
    for full in (left, left.T):
        high = full.astype(ml_dtypes.bfloat16)
        low = (full - high.astype(np.float32)).astype(ml_dtypes.bfloat16)
        stacks += [high, low]
    return [jnp.asarray(stack) for stack in stacks]


def dot(left, right):
    return jnp.dot(left, right, preferred_element_type=jnp.float32)


def split(full):
    high = full.astype(jnp.bfloat16)
    return high, (full - high.astype(jnp.float32)).astype(jnp.bfloat16)


def transform(real, imag, left_high, left_low, right_high, right_low):
    width = real.shape[0]
    high, low = split(jnp.concatenate([real, imag], axis=0))
    rows = dot(left_high, high) + dot(left_high, low) + dot(left_low, high)
    high, low = split(jnp.concatenate([rows[:width], rows[width:]], axis=1))
    cols = dot(high, right_high) + dot(low, right_high) + dot(high, right_low)
    return cols[:, :width], cols[:, width:]


def visit_kernel(offs, ext, probe, coeffs, pats, ah, al, bh, bl, grad, stats, shifted):
    width = probe.shape[1]
    size = ext.shape[1]
    tile = size - width
    grad[...] = jnp.zeros_like(grad)
    stats[...] = jnp.zeros_like(stats)
    shifted[...] = jnp.zeros_like(shifted)

    def visit(p, carry):
        oy, ox = offs[p, 0], offs[p, 1]
        odd = lax.rem(oy, 8)
        even = pl.multiple_of(oy - odd, 8)
        window = []
        for part in (0, 1):
            rows = pltpu.roll(ext[part, pl.ds(even, width + 8), :], lax.rem(size - ox, size), axis=1)
            rows = pltpu.roll(rows[:, :width], lax.rem(width + 8 - odd, width + 8), axis=0)
            window.append(rows[:width])
        pr, pi = probe[0], probe[1]
        wr, wi = transform(
            pr * window[0] - pi * window[1],
            pr * window[1] + pi * window[0],
            ah[...], al[...], bh[...], bl[...],
        )
        inten = wr * wr + wi * wi
        lin, quad, cubic = coeffs[0], coeffs[1], coeffs[2]
        error = inten * (lin + inten * (quad + inten * cubic)) - pats[p]
        weight = 2.0 * error * (lin + inten * (2.0 * quad + 3.0 * cubic * inten))
        squared = inten * inten
        cubed = squared * inten
        stats[0] += error * inten
        stats[1] += error * squared
        stats[2] += error * cubed
        stats[3] += squared
        stats[4] += squared * squared
        stats[5] += cubed * cubed
        br, bi = transform(weight * wr, weight * wi, bh[...], bl[...], ah[...], al[...])
        below = jnp.zeros((8, width), jnp.float32)
        beside = jnp.zeros((width + 8, tile), jnp.float32)
        for part, g in ((0, pr * br + pi * bi), (1, pr * bi - pi * br)):
            g = pltpu.roll(jnp.concatenate([g, below], axis=0), odd, axis=0)
            g = pltpu.roll(jnp.concatenate([g, beside], axis=1), ox, axis=1)
            shifted[part, tile : tile + width + 8, :] = g
            grad[part] += shifted[part, pl.ds(pl.multiple_of(tile - even, 8), size), :]
        return carry

    lax.fori_loop(0, pats.shape[0], visit, 0)


def visit_windows(offs, ext, probe, coeffs, pats, stacks):
    width = probe.shape[1]
    size = ext.shape[1]
    vmem = pl.BlockSpec(memory_space=pltpu.VMEM)
    return pl.pallas_call(
        visit_kernel,
        out_shape=(
            jax.ShapeDtypeStruct(ext.shape, jnp.float32),
            jax.ShapeDtypeStruct((6, width, width), jnp.float32),
        ),
        in_specs=[pl.BlockSpec(memory_space=pltpu.SMEM)] + [vmem] * 8,
        out_specs=(vmem, vmem),
        scratch_shapes=[pltpu.VMEM((2, 2 * (size - width) + width, size), jnp.float32)],
        compiler_params=pltpu.CompilerParams(vmem_limit_bytes=40 * 1024 * 1024),
        name="visit_windows",
    )(offs, ext, probe, coeffs, pats, *stacks)


def fold_rows(grad_ext, half):
    received = []
    for toward, border in ((-1, grad_ext[:, :half, :]), (1, grad_ext[:, -half:, :])):
        received.append(passed_along(border, "row", toward))
    middle = grad_ext[:, half:-half, :]
    return middle.at[:, -half:, :].add(received[0]).at[:, :half, :].add(received[1])


def fold_cols(grad_mid, half):
    received = []
    for toward, border in ((-1, grad_mid[:, :, :half]), (1, grad_mid[:, :, -half:])):
        received.append(passed_along(border, "col", toward))
    middle = grad_mid[:, :, half:-half]
    return middle.at[:, :, -half:].add(received[0]).at[:, :, :half].add(received[1])


def local(object_field, probe, coeffs, patterns, offsets):
    width = probe.shape[1]
    half = width // 2
    tile = object_field.shape[1]
    stacks = dft_stacks(width)
    flat_pats = patterns.reshape(-1, width, width)
    flat_offs = offsets.reshape(-1, 2)
    devices = lax.axis_size("row") * lax.axis_size("col")
    total = 2.0 * tile * tile * devices
    for turn in range(ITERS):
        extended = padded(object_field, (("row", 1), ("col", 2)), half)
        grad_ext, stats = visit_windows(flat_offs, extended, probe, coeffs, flat_pats, stacks)
        stats = lax.psum(stats, ("row", "col"))
        new_coeffs = coeffs - stats[:3] / (stats[3:] + RIDGE)
        grad = fold_cols(fold_rows(grad_ext, half), half)
        sumsq = lax.psum(jnp.sum(grad * grad), ("row", "col"))
        object_field = object_field - STEP_RATE * grad / jnp.sqrt(sumsq / total + EPSILON)
        coeffs = new_coeffs
    return (object_field, coeffs)


def solution(mesh):
    placed = (
        P(None, "row", "col"),
        P(),
        P(),
        P("row", "col", None, None, None),
        P("row", "col", None, None),
    )
    return jax.shard_map(
        local, mesh=mesh, in_specs=placed, out_specs=(P(None, "row", "col"), P()), check_vma=False
    )
```

```python
import functools

import jax
import jax.numpy as jnp
import ml_dtypes
import numpy as np
from jax import lax
from jax.experimental import pallas as pl
from jax.experimental.pallas import tpu as pltpu
from jax.sharding import PartitionSpec as P

ITERS = 2


STEP_RATE = 0.2
RIDGE = 1.0
EPSILON = 1e-06


def dft_stacks(order):
    index = np.arange(order)
    angle = -2.0 * np.pi / order * (index[:, None] * index[None, :] % order)
    real, imag = np.cos(angle) / np.sqrt(order), np.sin(angle) / np.sqrt(order)
    left = np.block([[real, -imag], [imag, real]]).astype(np.float32)
    stacks = []
    for full in (left, left.T):
        high = full.astype(ml_dtypes.bfloat16)
        low = (full - high.astype(np.float32)).astype(ml_dtypes.bfloat16)
        stacks += [high, low]
    return [jnp.asarray(stack) for stack in stacks]


def dot(left, right):
    return jnp.dot(left, right, preferred_element_type=jnp.float32)


def split(full):
    high = full.astype(jnp.bfloat16)
    return high, (full - high.astype(jnp.float32)).astype(jnp.bfloat16)


def transform(real, imag, left_high, left_low, right_high, right_low):
    width = real.shape[0]
    high, low = split(jnp.concatenate([real, imag], axis=0))
    rows = dot(left_high, high) + dot(left_high, low) + dot(left_low, high)
    high, low = split(jnp.concatenate([rows[:width], rows[width:]], axis=1))
    cols = dot(high, right_high) + dot(low, right_high) + dot(high, right_low)
    return cols[:, :width], cols[:, width:]


def visit_kernel(offs, ext, probe, coeffs, pats, ah, al, bh, bl, grad, stats, shifted):
    width = probe.shape[1]
    size = ext.shape[1]
    tile = size - width
    grad[...] = jnp.zeros_like(grad)
    stats[...] = jnp.zeros_like(stats)
    shifted[...] = jnp.zeros_like(shifted)

    def visit(p, carry):
        oy, ox = offs[p, 0], offs[p, 1]
        odd = lax.rem(oy, 8)
        even = pl.multiple_of(oy - odd, 8)
        window = []
        for part in (0, 1):
            rows = pltpu.roll(ext[part, pl.ds(even, width + 8), :], lax.rem(size - ox, size), axis=1)
            rows = pltpu.roll(rows[:, :width], lax.rem(width + 8 - odd, width + 8), axis=0)
            window.append(rows[:width])
        pr, pi = probe[0], probe[1]
        wr, wi = transform(
            pr * window[0] - pi * window[1],
            pr * window[1] + pi * window[0],
            ah[...], al[...], bh[...], bl[...],
        )
        inten = wr * wr + wi * wi
        lin, quad, cubic = coeffs[0], coeffs[1], coeffs[2]
        error = inten * (lin + inten * (quad + inten * cubic)) - pats[p]
        weight = 2.0 * error * (lin + inten * (2.0 * quad + 3.0 * cubic * inten))
        squared = inten * inten
        cubed = squared * inten
        stats[0] += error * inten
        stats[1] += error * squared
        stats[2] += error * cubed
        stats[3] += squared
        stats[4] += squared * squared
        stats[5] += cubed * cubed
        br, bi = transform(weight * wr, weight * wi, bh[...], bl[...], ah[...], al[...])
        below = jnp.zeros((8, width), jnp.float32)
        beside = jnp.zeros((width + 8, tile), jnp.float32)
        for part, g in ((0, pr * br + pi * bi), (1, pr * bi - pi * br)):
            g = pltpu.roll(jnp.concatenate([g, below], axis=0), odd, axis=0)
            g = pltpu.roll(jnp.concatenate([g, beside], axis=1), ox, axis=1)
            shifted[part, tile : tile + width + 8, :] = g
            grad[part] += shifted[part, pl.ds(pl.multiple_of(tile - even, 8), size), :]
        return carry

    lax.fori_loop(0, pats.shape[0], visit, 0)


def visit_windows(offs, ext, probe, coeffs, pats, stacks):
    width = probe.shape[1]
    size = ext.shape[1]
    vmem = pl.BlockSpec(memory_space=pltpu.VMEM)
    return pl.pallas_call(
        visit_kernel,
        out_shape=(
            jax.ShapeDtypeStruct(ext.shape, jnp.float32),
            jax.ShapeDtypeStruct((6, width, width), jnp.float32),
        ),
        in_specs=[pl.BlockSpec(memory_space=pltpu.SMEM)] + [vmem] * 8,
        out_specs=(vmem, vmem),
        scratch_shapes=[pltpu.VMEM((2, 2 * (size - width) + width, size), jnp.float32)],
        compiler_params=pltpu.CompilerParams(vmem_limit_bytes=40 * 1024 * 1024),
        name="visit_windows",
    )(offs, ext, probe, coeffs, pats, *stacks)


class Link:
    def __init__(self, axis, step, source, target, sems, slot):
        self.axis, self.step = axis, step
        here, count = lax.axis_index(axis), lax.axis_size(axis)
        self.copy = remote(
            source, target, sems, slot, {axis: lax.rem(here + step + count, count)}
        )

    def exists(self, step):
        here, count = lax.axis_index(self.axis), lax.axis_size(self.axis)
        return here > 0 if step < 0 else here < count - 1

    def start(self):
        pl.when(self.exists(self.step))(self.copy.start)
        return self

    def arrived(self, then=None):
        @pl.when(self.exists(-self.step))
        def _():
            self.copy.wait_recv()
            if then is not None:
                then()

    def sent(self):
        pl.when(self.exists(self.step))(self.copy.wait_send)


def remote(source, target, sems, slot, device):
    send, recv = sems
    where = tuple(device.get(axis, lax.axis_index(axis)) for axis in ("row", "col"))
    return pltpu.make_async_remote_copy(
        src_ref=source,
        dst_ref=target,
        send_sem=send.at[slot],
        recv_sem=recv.at[slot],
        device_id=where,
        device_id_type=pl.DeviceIdType.MESH,
    )


def greet():
    barrier = pltpu.get_barrier_semaphore()
    count = 0
    for axis in ("row", "col"):
        size = lax.axis_size(axis)
        here = lax.axis_index(axis)
        for distance in range(1, size):
            other = {"row": lax.axis_index("row"), "col": lax.axis_index("col")}
            other[axis] = lax.rem(here + distance, size)
            pl.semaphore_signal(
                barrier,
                inc=1,
                device_id=(other["row"], other["col"]),
                device_id_type=pl.DeviceIdType.MESH,
            )
            count += 1
    pl.semaphore_wait(barrier, count)


class Slots:
    def __init__(self, sems):
        self.sems, self.used = sems, 0

    def next(self):
        self.used += 1
        return self.used - 1


def copies_needed():
    rows, cols = lax.axis_size("row"), lax.axis_size("col")
    return 2 * (1 + cols + rows // 2) + cols + rows + 8


def halo_cols(field, half, tile, slots):
    inner = pl.ds(half, tile)
    return [
        Link("col", -1, field.at[:, inner, half : 2 * half],
             field.at[:, inner, half + tile :], slots.sems, slots.next()).start(),
        Link("col", 1, field.at[:, inner, tile : half + tile],
             field.at[:, inner, :half], slots.sems, slots.next()).start(),
    ]


def halo_rows(field, half, tile, slots):
    return [
        Link("row", -1, field.at[:, half : 2 * half, :],
             field.at[:, half + tile :, :], slots.sems, slots.next()).start(),
        Link("row", 1, field.at[:, tile : half + tile, :],
             field.at[:, :half, :], slots.sems, slots.next()).start(),
    ]


def update_kernel(last, grad, stats, field, coeffs, field_out, coeffs_out,
                  gfull, from_rows, mid, from_cols, half_sums, col_sums, shard, z_sums,
                  new_coeffs, sq_mine, sq_cols, sq_part, sq_rows, send, recv):
    rows, cols = lax.axis_size("row"), lax.axis_size("col")
    r, c = lax.axis_index("row"), lax.axis_index("col")
    depth = rows // 2
    k, z = lax.rem(r, 2), lax.div(r, 2)
    width = stats.shape[1]
    half = width // 2
    tile = grad.shape[1] - width
    slots = Slots((send, recv))
    rows1, rows2, rows3 = half_sums.shape[1], shard.shape[1], z_sums.shape[2]
    cut = rows3 < rows2

    gfull[...] = jnp.zeros_like(gfull)
    greet()

    def at(start, size):
        return pl.ds(pl.multiple_of(start, 8), size)

    def to(source, target, device):
        copy = remote(source, target, slots.sems, slots.next(), device)
        copy.start()
        return copy

    waiting = []
    low = Link("row", -1, grad.at[:, :half, :], from_rows.at[0], slots.sems, slots.next()).start()
    high = Link("row", 1, grad.at[:, half + tile :, :], from_rows.at[1], slots.sems, slots.next()).start()
    waiting += [low.sent, high.sent]
    partner = {"row": r + 1 - 2 * k}
    pair = to(stats.at[:, at((1 - k) * rows1, rows1), :], half_sums, partner)
    waiting.append(pair.wait_send)

    mid[...] = grad[:, half : half + tile, :]

    def add_low():
        mid[:, tile - half :, :] += from_rows[0]

    def add_high():
        mid[:, :half, :] += from_rows[1]

    low.arrived(add_low)
    high.arrived(add_high)
    low = Link("col", -1, mid.at[:, :, :half], from_cols.at[0], slots.sems, slots.next()).start()
    high = Link("col", 1, mid.at[:, :, half + tile :], from_cols.at[1], slots.sems, slots.next()).start()
    waiting += [low.sent, high.sent]

    pair.wait_recv()
    half_sums[...] += stats[:, at(k * rows1, rows1), :]
    over_cols = []
    for d in range(1, cols):
        other = lax.rem(c + d, cols)
        over_cols.append(
            to(half_sums.at[:, at(other * rows2, rows2), :], col_sums.at[d - 1], {"col": other})
        )

    inner = pl.ds(half, tile)
    gfull[:, inner, half : half + tile] = mid[:, :, half : half + tile]

    def add_low():
        gfull[:, inner, tile : half + tile] += from_cols[0]

    def add_high():
        gfull[:, inner, half : 2 * half] += from_cols[1]

    low.arrived(add_low)
    high.arrived(add_high)
    if not last:
        links = halo_cols(gfull, half, tile, slots)
    mine = gfull[:, inner, half : half + tile]
    square = jnp.sum(mine * mine, axis=0)
    square = jnp.sum(square.reshape(-1, 8, tile), axis=0)
    sq_mine[...] = sum(square[:, i : i + 128] for i in range(0, tile, 128))
    sq_over_cols = [
        to(sq_mine, sq_cols.at[d - 1], {"col": lax.rem(c + d, cols)}) for d in range(1, cols)
    ]
    for copy in sq_over_cols:
        copy.wait_recv()
    sq_part[...] = sq_mine[...] + sum(sq_cols[d] for d in range(cols - 1))
    sq_over_rows = [
        to(sq_part, sq_rows.at[d - 1], {"row": lax.rem(r + d, rows)}) for d in range(1, rows)
    ]
    if not last:
        for link in links:
            link.arrived()
        waiting += [link.sent for link in links]
        links = halo_rows(gfull, half, tile, slots)
        waiting += [link.sent for link in links]

    for copy in over_cols:
        copy.wait_recv()
    shard[...] = half_sums[:, at(c * rows2, rows2), :] + sum(col_sums[d] for d in range(cols - 1))
    over_z = []
    for d in range(1, depth):
        other = lax.rem(z + d, depth)
        source = shard.at[:, at(other * rows3, rows3), :] if cut else shard
        over_z.append(to(source, z_sums.at[z], {"row": 2 * other + k}))
    z_sums[z] = shard[:, at(z * rows3, rows3), :] if cut else shard[...]
    for copy in over_z:
        copy.wait_recv()
    sums = sum(z_sums[i] for i in range(depth))
    base2 = k * rows1 + c * rows2
    base3 = base2 + z * rows3 if cut else base2
    new_coeffs[:, at(base3, rows3), :] = coeffs[:, at(base3, rows3), :] - sums[:3] / (sums[3:] + RIDGE)
    back = []
    if cut:
        ready = new_coeffs.at[:, at(base3, rows3), :]
        for d in range(1, depth):
            back.append(to(ready, ready, {"row": 2 * lax.rem(z + d, depth) + k}))
        for copy in back:
            copy.wait_recv()
    ready = new_coeffs.at[:, at(base2, rows2), :]
    wide = [to(ready, ready, {"col": lax.rem(c + d, cols)}) for d in range(1, cols)]
    for copy in wide:
        copy.wait_recv()
    ready = new_coeffs.at[:, at(k * rows1, rows1), :]
    pair = to(ready, ready, partner)

    for copy in sq_over_rows:
        copy.wait_recv()
    square = sq_part[...] + sum(sq_rows[d] for d in range(rows - 1))
    total = 2.0 * tile * tile * rows * cols
    rate = STEP_RATE / jnp.sqrt(jnp.sum(square, keepdims=True) / total + EPSILON)
    if last:
        for part in (0, 1):
            field_out[part] = field[part, inner, half : half + tile] - rate * gfull[part, inner, half : half + tile]
    else:
        for link in links:
            link.arrived()
        for part in (0, 1):
            field_out[part] = field[part] - rate * gfull[part]
    pair.wait()
    coeffs_out[...] = new_coeffs[...]
    for done in waiting:
        done()
    for copy in over_cols + sq_over_cols + sq_over_rows + over_z + back + wide:
        copy.wait_send()


def update(last, grad, stats, field, coeffs):
    rows, cols = lax.axis_size("row"), lax.axis_size("col")
    depth = rows // 2
    size, width = grad.shape[1], stats.shape[1]
    half, tile = width // 2, size - width
    rows1 = width // 2
    rows2 = rows1 // cols
    rows3 = rows2 // depth if rows2 % (8 * depth) == 0 else rows2
    vmem = pl.BlockSpec(memory_space=pltpu.VMEM)
    f32 = jnp.float32
    count = copies_needed()
    side = tile if last else size
    return pl.pallas_call(
        functools.partial(update_kernel, last),
        out_shape=(
            jax.ShapeDtypeStruct((2, side, side), f32),
            jax.ShapeDtypeStruct(coeffs.shape, f32),
        ),
        in_specs=[vmem] * 4,
        out_specs=(vmem, vmem),
        scratch_shapes=[
            pltpu.VMEM((2, size, size), f32),
            pltpu.VMEM((2, 2, half, size), f32),
            pltpu.VMEM((2, tile, size), f32),
            pltpu.VMEM((2, 2, tile, half), f32),
            pltpu.VMEM((6, rows1, width), f32),
            pltpu.VMEM((cols - 1, 6, rows2, width), f32),
            pltpu.VMEM((6, rows2, width), f32),
            pltpu.VMEM((depth, 6, rows3, width), f32),
            pltpu.VMEM(coeffs.shape, f32),
            pltpu.VMEM((8, 128), f32),
            pltpu.VMEM((cols - 1, 8, 128), f32),
            pltpu.VMEM((8, 128), f32),
            pltpu.VMEM((rows - 1, 8, 128), f32),
            pltpu.SemaphoreType.DMA((count,)),
            pltpu.SemaphoreType.DMA((count,)),
        ],
        compiler_params=pltpu.CompilerParams(
            collective_id=2 if last else 1,
            has_side_effects=True,
            vmem_limit_bytes=48 * 1024 * 1024,
        ),
        name="update_last" if last else "update",
    )(grad, stats, field, coeffs)


def extend_kernel(half, tile, field, out, full, send, recv):
    full[...] = jnp.zeros_like(full)
    inner = pl.ds(half, tile)
    full[:, inner, half : half + tile] = field[...]
    barrier = pltpu.get_barrier_semaphore()
    count = jnp.int32(0)
    for axis in ("row", "col"):
        size = lax.axis_size(axis)
        here = lax.axis_index(axis)
        for step in (-1, 1):
            other = {"row": lax.axis_index("row"), "col": lax.axis_index("col")}
            other[axis] = lax.rem(here + step + size, size)
            exists = here > 0 if step < 0 else here < size - 1
            count += exists.astype(jnp.int32)

            @pl.when(exists)
            def _():
                pl.semaphore_signal(
                    barrier,
                    inc=1,
                    device_id=(other["row"], other["col"]),
                    device_id_type=pl.DeviceIdType.MESH,
                )

    pl.semaphore_wait(barrier, count)
    slots = Slots((send, recv))
    side = halo_cols(full, half, tile, slots)
    for link in side:
        link.arrived()
    ends = halo_rows(full, half, tile, slots)
    for link in ends:
        link.arrived()
    out[...] = full[...]
    for link in side + ends:
        link.sent()


def extend(field, half):
    tile = field.shape[1]
    size = tile + 2 * half
    vmem = pl.BlockSpec(memory_space=pltpu.VMEM)
    return pl.pallas_call(
        functools.partial(extend_kernel, half, tile),
        out_shape=jax.ShapeDtypeStruct((2, size, size), jnp.float32),
        in_specs=[vmem],
        out_specs=vmem,
        scratch_shapes=[
            pltpu.VMEM((2, size, size), jnp.float32),
            pltpu.SemaphoreType.DMA((4,)),
            pltpu.SemaphoreType.DMA((4,)),
        ],
        compiler_params=pltpu.CompilerParams(
            collective_id=0, has_side_effects=True, vmem_limit_bytes=32 * 1024 * 1024
        ),
        name="extend",
    )(field)


def local(object_field, probe, coeffs, patterns, offsets):
    width = probe.shape[1]
    stacks = dft_stacks(width)
    flat_pats = patterns.reshape(-1, width, width)
    flat_offs = offsets.reshape(-1, 2)
    field = extend(object_field, width // 2)
    for turn in range(ITERS):
        grad, stats = visit_windows(flat_offs, field, probe, coeffs, flat_pats, stacks)
        field, coeffs = update(turn == ITERS - 1, grad, stats, field, coeffs)
    return (field, coeffs)


def solution(mesh):
    placed = (
        P(None, "row", "col"),
        P(),
        P(),
        P("row", "col", None, None, None),
        P("row", "col", None, None),
    )
    return jax.shard_map(
        local, mesh=mesh, in_specs=placed, out_specs=(P(None, "row", "col"), P()), check_vma=False
    )
```

```python
import functools

import jax
import jax.numpy as jnp
import ml_dtypes
import numpy as np
from jax import lax
from jax.experimental import pallas as pl
from jax.experimental.pallas import tpu as pltpu
from jax.sharding import PartitionSpec as P

ITERS = 2


STEP_RATE = 0.2
RIDGE = 1.0
EPSILON = 1e-06


def dft_stacks(order):
    index = np.arange(order)
    angle = -2.0 * np.pi / order * (index[:, None] * index[None, :] % order)
    real, imag = np.cos(angle) / np.sqrt(order), np.sin(angle) / np.sqrt(order)
    left = np.block([[real, -imag], [imag, real]]).astype(np.float32)
    stacks = []
    for full in (left, left.T):
        high = full.astype(ml_dtypes.bfloat16)
        low = (full - high.astype(np.float32)).astype(ml_dtypes.bfloat16)
        stacks += [high, low]
    return [jnp.asarray(stack) for stack in stacks]


def dot(left, right):
    return jnp.dot(left, right, preferred_element_type=jnp.float32)


def split(full):
    high = full.astype(jnp.bfloat16)
    return high, (full - high.astype(jnp.float32)).astype(jnp.bfloat16)


def transform(real, imag, left_high, left_low, right_high, right_low):
    width = real.shape[0]
    high, low = split(jnp.concatenate([real, imag], axis=0))
    rows = dot(left_high, high) + dot(left_high, low) + dot(left_low, high)
    high, low = split(jnp.concatenate([rows[:width], rows[width:]], axis=1))
    cols = dot(high, right_high) + dot(low, right_high) + dot(high, right_low)
    return cols[:, :width], cols[:, width:]


def visit_kernel(offs, ext, probe, coeffs, pats, ah, al, bh, bl, grad, stats, shifted):
    width = probe.shape[1]
    size = ext.shape[1]
    tile = size - width
    grad[...] = jnp.zeros_like(grad)
    stats[...] = jnp.zeros_like(stats)
    shifted[...] = jnp.zeros_like(shifted)

    def visit(p, carry):
        oy, ox = offs[p, 0], offs[p, 1]
        odd = lax.rem(oy, 8)
        even = pl.multiple_of(oy - odd, 8)
        window = []
        for part in (0, 1):
            rows = pltpu.roll(ext[part, pl.ds(even, width + 8), :], lax.rem(size - ox, size), axis=1)
            rows = pltpu.roll(rows[:, :width], lax.rem(width + 8 - odd, width + 8), axis=0)
            window.append(rows[:width])
        pr, pi = probe[0], probe[1]
        wr, wi = transform(
            pr * window[0] - pi * window[1],
            pr * window[1] + pi * window[0],
            ah[...], al[...], bh[...], bl[...],
        )
        inten = wr * wr + wi * wi
        lin, quad, cubic = coeffs[0], coeffs[1], coeffs[2]
        error = inten * (lin + inten * (quad + inten * cubic)) - pats[p]
        weight = 2.0 * error * (lin + inten * (2.0 * quad + 3.0 * cubic * inten))
        squared = inten * inten
        cubed = squared * inten
        stats[0] += error * inten
        stats[1] += error * squared
        stats[2] += error * cubed
        stats[3] += squared
        stats[4] += squared * squared
        stats[5] += cubed * cubed
        br, bi = transform(weight * wr, weight * wi, bh[...], bl[...], ah[...], al[...])
        below = jnp.zeros((8, width), jnp.float32)
        beside = jnp.zeros((width + 8, tile), jnp.float32)
        for part, g in ((0, pr * br + pi * bi), (1, pr * bi - pi * br)):
            g = pltpu.roll(jnp.concatenate([g, below], axis=0), odd, axis=0)
            g = pltpu.roll(jnp.concatenate([g, beside], axis=1), ox, axis=1)
            shifted[part, tile : tile + width + 8, :] = g
            grad[part] += shifted[part, pl.ds(pl.multiple_of(tile - even, 8), size), :]
        return carry

    lax.fori_loop(0, pats.shape[0], visit, 0)


def visit_windows(offs, ext, probe, coeffs, pats, stacks):
    width = probe.shape[1]
    size = ext.shape[1]
    vmem = pl.BlockSpec(memory_space=pltpu.VMEM)
    return pl.pallas_call(
        visit_kernel,
        out_shape=(
            jax.ShapeDtypeStruct(ext.shape, jnp.float32),
            jax.ShapeDtypeStruct((6, width, width), jnp.float32),
        ),
        in_specs=[pl.BlockSpec(memory_space=pltpu.SMEM)] + [vmem] * 8,
        out_specs=(vmem, vmem),
        scratch_shapes=[pltpu.VMEM((2, 2 * (size - width) + width, size), jnp.float32)],
        compiler_params=pltpu.CompilerParams(vmem_limit_bytes=40 * 1024 * 1024),
        name="visit_windows",
    )(offs, ext, probe, coeffs, pats, *stacks)


class Link:
    def __init__(self, axis, step, source, target, sems, slot):
        self.axis, self.step = axis, step
        here, count = lax.axis_index(axis), lax.axis_size(axis)
        self.copy = remote(
            source, target, sems, slot, {axis: lax.rem(here + step + count, count)}
        )

    def exists(self, step):
        here, count = lax.axis_index(self.axis), lax.axis_size(self.axis)
        return here > 0 if step < 0 else here < count - 1

    def start(self):
        pl.when(self.exists(self.step))(self.copy.start)
        return self

    def arrived(self, then=None):
        @pl.when(self.exists(-self.step))
        def _():
            self.copy.wait_recv()
            if then is not None:
                then()

    def sent(self):
        pl.when(self.exists(self.step))(self.copy.wait_send)


def remote(source, target, sems, slot, device):
    send, recv = sems
    where = tuple(device.get(axis, lax.axis_index(axis)) for axis in ("row", "col"))
    return pltpu.make_async_remote_copy(
        src_ref=source,
        dst_ref=target,
        send_sem=send.at[slot],
        recv_sem=recv.at[slot],
        device_id=where,
        device_id_type=pl.DeviceIdType.MESH,
    )


def greet():
    barrier = pltpu.get_barrier_semaphore()
    count = 0
    for axis in ("row", "col"):
        size = lax.axis_size(axis)
        here = lax.axis_index(axis)
        for distance in range(1, size):
            other = {"row": lax.axis_index("row"), "col": lax.axis_index("col")}
            other[axis] = lax.rem(here + distance, size)
            pl.semaphore_signal(
                barrier,
                inc=1,
                device_id=(other["row"], other["col"]),
                device_id_type=pl.DeviceIdType.MESH,
            )
            count += 1
    pl.semaphore_wait(barrier, count)


class Slots:
    def __init__(self, sems):
        self.sems, self.used = sems, 0

    def next(self):
        self.used += 1
        return self.used - 1


def copies_needed():
    rows, cols = lax.axis_size("row"), lax.axis_size("col")
    return 2 * (1 + cols + rows // 2) + cols + rows + 16


def halo_cols(field, part, half, tile, slots):
    inner = pl.ds(half, tile)
    return [
        Link("col", -1, field.at[part, inner, half : 2 * half],
             field.at[part, inner, half + tile :], slots.sems, slots.next()).start(),
        Link("col", 1, field.at[part, inner, tile : half + tile],
             field.at[part, inner, :half], slots.sems, slots.next()).start(),
    ]


def halo_rows(field, part, half, tile, slots):
    return [
        Link("row", -1, field.at[part, half : 2 * half, :],
             field.at[part, half + tile :, :], slots.sems, slots.next()).start(),
        Link("row", 1, field.at[part, tile : half + tile, :],
             field.at[part, :half, :], slots.sems, slots.next()).start(),
    ]


def fold_rows(grad, into, part, half, tile, slots):
    return [
        Link("row", -1, grad.at[part, :half, :], into.at[0, part], slots.sems, slots.next()).start(),
        Link("row", 1, grad.at[part, half + tile :, :], into.at[1, part], slots.sems, slots.next()).start(),
    ]


def fold_cols(mid, into, part, half, tile, slots):
    return [
        Link("col", -1, mid.at[part, :, :half], into.at[0, part], slots.sems, slots.next()).start(),
        Link("col", 1, mid.at[part, :, half + tile :], into.at[1, part], slots.sems, slots.next()).start(),
    ]


def update_kernel(last, grad, stats, field, coeffs, field_out, coeffs_out,
                  gfull, from_rows, mid, from_cols, half_sums, col_sums, shard, z_sums,
                  new_coeffs, sq_mine, sq_cols, sq_part, sq_rows, send_sem, recv_sem):
    rows, cols = lax.axis_size("row"), lax.axis_size("col")
    r, c = lax.axis_index("row"), lax.axis_index("col")
    depth = rows // 2
    k, z = lax.rem(r, 2), lax.div(r, 2)
    width = stats.shape[1]
    half = width // 2
    tile = grad.shape[1] - width
    slots = Slots((send_sem, recv_sem))
    rows1, rows2, rows3 = half_sums.shape[1], shard.shape[1], z_sums.shape[2]
    cut = rows3 < rows2

    gfull[...] = jnp.zeros_like(gfull)
    greet()

    def at(start, size):
        return pl.ds(pl.multiple_of(start, 8), size)

    def to(source, target, device):
        copy = remote(source, target, slots.sems, slots.next(), device)
        copy.start()
        return copy

    links = []

    def send(start, *refs):
        pair = start(*refs, half, tile, slots)
        links.extend(pair)
        return pair

    row_links = [send(fold_rows, grad, from_rows, part) for part in (0, 1)]
    partner = {"row": r + 1 - 2 * k}
    pair = to(stats.at[:, at((1 - k) * rows1, rows1), :], half_sums, partner)
    mid[...] = grad[:, half : half + tile, :]

    pair.wait_recv()
    half_sums[...] += stats[:, at(k * rows1, rows1), :]
    over_cols = []
    for d in range(1, cols):
        other = lax.rem(c + d, cols)
        over_cols.append(
            to(half_sums.at[:, at(other * rows2, rows2), :], col_sums.at[d - 1], {"col": other})
        )

    col_links = []
    for part in (0, 1):
        def add_low():
            mid[part, tile - half :, :] += from_rows[0, part]

        def add_high():
            mid[part, :half, :] += from_rows[1, part]

        row_links[part][0].arrived(add_low)
        row_links[part][1].arrived(add_high)
        col_links.append(send(fold_cols, mid, from_cols, part))

    for copy in over_cols:
        copy.wait_recv()
    shard[...] = half_sums[:, at(c * rows2, rows2), :] + sum(col_sums[d] for d in range(cols - 1))
    over_z = []
    for d in range(1, depth):
        other = lax.rem(z + d, depth)
        source = shard.at[:, at(other * rows3, rows3), :] if cut else shard
        over_z.append(to(source, z_sums.at[z], {"row": 2 * other + k}))
    z_sums[z] = shard[:, at(z * rows3, rows3), :] if cut else shard[...]

    inner = pl.ds(half, tile)
    side_links = []
    square = 0.0
    for part in (0, 1):
        gfull[part, inner, half : half + tile] = mid[part, :, half : half + tile]

        def add_low():
            gfull[part, inner, tile : half + tile] += from_cols[0, part]

        def add_high():
            gfull[part, inner, half : 2 * half] += from_cols[1, part]

        col_links[part][0].arrived(add_low)
        col_links[part][1].arrived(add_high)
        if not last:
            side_links.append(send(halo_cols, gfull, part))
        mine = gfull[part, inner, half : half + tile]
        square += jnp.sum((mine * mine).reshape(-1, 8, tile), axis=0)
    sq_mine[...] = sum(square[:, i : i + 128] for i in range(0, tile, 128))
    sq_over_cols = [
        to(sq_mine, sq_cols.at[d - 1], {"col": lax.rem(c + d, cols)}) for d in range(1, cols)
    ]

    for copy in over_z:
        copy.wait_recv()
    sums = sum(z_sums[i] for i in range(depth))
    base2 = k * rows1 + c * rows2
    base3 = base2 + z * rows3 if cut else base2
    new_coeffs[:, at(base3, rows3), :] = coeffs[:, at(base3, rows3), :] - sums[:3] / (sums[3:] + RIDGE)
    back = []
    if cut:
        ready = new_coeffs.at[:, at(base3, rows3), :]
        for d in range(1, depth):
            back.append(to(ready, ready, {"row": 2 * lax.rem(z + d, depth) + k}))

    for copy in sq_over_cols:
        copy.wait_recv()
    sq_part[...] = sq_mine[...] + sum(sq_cols[d] for d in range(cols - 1))
    sq_over_rows = [
        to(sq_part, sq_rows.at[d - 1], {"row": lax.rem(r + d, rows)}) for d in range(1, rows)
    ]

    end_links = []
    if not last:
        for part in (0, 1):
            for link in side_links[part]:
                link.arrived()
            end_links.append(send(halo_rows, gfull, part))
    for copy in back:
        copy.wait_recv()
    ready = new_coeffs.at[:, at(base2, rows2), :]
    wide = [to(ready, ready, {"col": lax.rem(c + d, cols)}) for d in range(1, cols)]

    for copy in sq_over_rows:
        copy.wait_recv()
    square = sq_part[...] + sum(sq_rows[d] for d in range(rows - 1))
    total = 2.0 * tile * tile * rows * cols
    rate = STEP_RATE / jnp.sqrt(jnp.sum(square, keepdims=True) / total + EPSILON)
    if last:
        for part in (0, 1):
            field_out[part] = field[part, inner, half : half + tile] - rate * gfull[part, inner, half : half + tile]

    for copy in wide:
        copy.wait_recv()
    ready = new_coeffs.at[:, at(k * rows1, rows1), :]
    final = to(ready, ready, partner)
    if not last:
        for part in (0, 1):
            for link in end_links[part]:
                link.arrived()
            field_out[part] = field[part] - rate * gfull[part]
    final.wait_recv()
    coeffs_out[...] = new_coeffs[...]
    for link in links:
        link.sent()
    for copy in [pair, final] + over_cols + sq_over_cols + sq_over_rows + over_z + back + wide:
        copy.wait_send()


def update(last, grad, stats, field, coeffs):
    rows, cols = lax.axis_size("row"), lax.axis_size("col")
    depth = rows // 2
    size, width = grad.shape[1], stats.shape[1]
    half, tile = width // 2, size - width
    rows1 = width // 2
    rows2 = rows1 // cols
    rows3 = rows2 // depth if rows2 % (8 * depth) == 0 else rows2
    vmem = pl.BlockSpec(memory_space=pltpu.VMEM)
    f32 = jnp.float32
    count = copies_needed()
    side = tile if last else size
    return pl.pallas_call(
        functools.partial(update_kernel, last),
        out_shape=(
            jax.ShapeDtypeStruct((2, side, side), f32),
            jax.ShapeDtypeStruct(coeffs.shape, f32),
        ),
        in_specs=[vmem] * 4,
        out_specs=(vmem, vmem),
        scratch_shapes=[
            pltpu.VMEM((2, size, size), f32),
            pltpu.VMEM((2, 2, half, size), f32),
            pltpu.VMEM((2, tile, size), f32),
            pltpu.VMEM((2, 2, tile, half), f32),
            pltpu.VMEM((6, rows1, width), f32),
            pltpu.VMEM((cols - 1, 6, rows2, width), f32),
            pltpu.VMEM((6, rows2, width), f32),
            pltpu.VMEM((depth, 6, rows3, width), f32),
            pltpu.VMEM(coeffs.shape, f32),
            pltpu.VMEM((8, 128), f32),
            pltpu.VMEM((cols - 1, 8, 128), f32),
            pltpu.VMEM((8, 128), f32),
            pltpu.VMEM((rows - 1, 8, 128), f32),
            pltpu.SemaphoreType.DMA((count,)),
            pltpu.SemaphoreType.DMA((count,)),
        ],
        compiler_params=pltpu.CompilerParams(
            collective_id=2 if last else 1,
            has_side_effects=True,
            vmem_limit_bytes=48 * 1024 * 1024,
        ),
        name="update_last" if last else "update",
    )(grad, stats, field, coeffs)


def extend_kernel(half, tile, field, out, full, send, recv):
    full[...] = jnp.zeros_like(full)
    inner = pl.ds(half, tile)
    full[:, inner, half : half + tile] = field[...]
    barrier = pltpu.get_barrier_semaphore()
    count = jnp.int32(0)
    for axis in ("row", "col"):
        size = lax.axis_size(axis)
        here = lax.axis_index(axis)
        for step in (-1, 1):
            other = {"row": lax.axis_index("row"), "col": lax.axis_index("col")}
            other[axis] = lax.rem(here + step + size, size)
            exists = here > 0 if step < 0 else here < size - 1
            count += exists.astype(jnp.int32)

            @pl.when(exists)
            def _():
                pl.semaphore_signal(
                    barrier,
                    inc=1,
                    device_id=(other["row"], other["col"]),
                    device_id_type=pl.DeviceIdType.MESH,
                )

    pl.semaphore_wait(barrier, count)
    slots = Slots((send, recv))
    side = [halo_cols(full, part, half, tile, slots) for part in (0, 1)]
    ends = []
    for part in (0, 1):
        for link in side[part]:
            link.arrived()
        ends.append(halo_rows(full, part, half, tile, slots))
    for part in (0, 1):
        for link in ends[part]:
            link.arrived()
    out[...] = full[...]
    for links in side + ends:
        for link in links:
            link.sent()


def extend(field, half):
    tile = field.shape[1]
    size = tile + 2 * half
    vmem = pl.BlockSpec(memory_space=pltpu.VMEM)
    return pl.pallas_call(
        functools.partial(extend_kernel, half, tile),
        out_shape=jax.ShapeDtypeStruct((2, size, size), jnp.float32),
        in_specs=[vmem],
        out_specs=vmem,
        scratch_shapes=[
            pltpu.VMEM((2, size, size), jnp.float32),
            pltpu.SemaphoreType.DMA((8,)),
            pltpu.SemaphoreType.DMA((8,)),
        ],
        compiler_params=pltpu.CompilerParams(
            collective_id=0, has_side_effects=True, vmem_limit_bytes=32 * 1024 * 1024
        ),
        name="extend",
    )(field)


def local(object_field, probe, coeffs, patterns, offsets):
    width = probe.shape[1]
    stacks = dft_stacks(width)
    flat_pats = patterns.reshape(-1, width, width)
    flat_offs = offsets.reshape(-1, 2)
    field = extend(object_field, width // 2)
    for turn in range(ITERS):
        grad, stats = visit_windows(flat_offs, field, probe, coeffs, flat_pats, stacks)
        field, coeffs = update(turn == ITERS - 1, grad, stats, field, coeffs)
    return (field, coeffs)


def solution(mesh):
    placed = (
        P(None, "row", "col"),
        P(),
        P(),
        P("row", "col", None, None, None),
        P("row", "col", None, None),
    )
    return jax.shard_map(
        local, mesh=mesh, in_specs=placed, out_specs=(P(None, "row", "col"), P()), check_vma=False
    )
```

```python
import functools

import jax
import jax.numpy as jnp
import ml_dtypes
import numpy as np
from jax import lax
from jax.experimental import pallas as pl
from jax.experimental.pallas import tpu as pltpu
from jax.sharding import PartitionSpec as P

ITERS = 2


STEP_RATE = 0.2
RIDGE = 1.0
EPSILON = 1e-06


def dft_stacks(order):
    index = np.arange(order)
    angle = -2.0 * np.pi / order * (index[:, None] * index[None, :] % order)
    real, imag = np.cos(angle) / np.sqrt(order), np.sin(angle) / np.sqrt(order)
    left = np.block([[real, -imag], [imag, real]]).astype(np.float32)
    stacks = []
    for full in (left, left.T):
        high = full.astype(ml_dtypes.bfloat16)
        low = (full - high.astype(np.float32)).astype(ml_dtypes.bfloat16)
        stacks += [high, low]
    return [jnp.asarray(stack) for stack in stacks]


def dot(left, right):
    return jnp.dot(left, right, preferred_element_type=jnp.float32)


def split(full):
    high = full.astype(jnp.bfloat16)
    return high, (full - high.astype(jnp.float32)).astype(jnp.bfloat16)


def transform(real, imag, left_high, left_low, right_high, right_low):
    width = real.shape[0]
    high, low = split(jnp.concatenate([real, imag], axis=0))
    rows = dot(left_high, high) + dot(left_high, low) + dot(left_low, high)
    high, low = split(jnp.concatenate([rows[:width], rows[width:]], axis=1))
    cols = dot(high, right_high) + dot(low, right_high) + dot(high, right_low)
    return cols[:, :width], cols[:, width:]


def visit_kernel(offs, ext, probe, coeffs, pats, ah, al, bh, bl, grad, stats):
    width = probe.shape[1]
    size = ext.shape[1]
    tile = size - width
    grad[...] = jnp.zeros_like(grad)
    stats[...] = jnp.zeros_like(stats)

    def visit(p, carry):
        oy, ox = offs[p, 0], offs[p, 1]
        odd = lax.rem(oy, 8)
        even = pl.multiple_of(oy - odd, 8)
        window = []
        for part in (0, 1):
            rows = pltpu.roll(ext[part, pl.ds(even, width + 8), :], lax.rem(size - ox, size), axis=1)
            rows = pltpu.roll(rows[:, :width], lax.rem(width + 8 - odd, width + 8), axis=0)
            window.append(rows[:width])
        pr, pi = probe[0], probe[1]
        wr, wi = transform(
            pr * window[0] - pi * window[1],
            pr * window[1] + pi * window[0],
            ah[...], al[...], bh[...], bl[...],
        )
        inten = wr * wr + wi * wi
        lin, quad, cubic = coeffs[0], coeffs[1], coeffs[2]
        error = inten * (lin + inten * (quad + inten * cubic)) - pats[p]
        weight = 2.0 * error * (lin + inten * (2.0 * quad + 3.0 * cubic * inten))
        squared = inten * inten
        cubed = squared * inten
        stats[0] += error * inten
        stats[1] += error * squared
        stats[2] += error * cubed
        stats[3] += squared
        stats[4] += squared * squared
        stats[5] += cubed * cubed
        br, bi = transform(weight * wr, weight * wi, bh[...], bl[...], ah[...], al[...])
        below = jnp.zeros((8, width), jnp.float32)
        beside = jnp.zeros((width + 8, tile), jnp.float32)
        for part, g in ((0, pr * br + pi * bi), (1, pr * bi - pi * br)):
            g = pltpu.roll(jnp.concatenate([g, below], axis=0), odd, axis=0)
            g = pltpu.roll(jnp.concatenate([g, beside], axis=1), ox, axis=1)
            grad[part, pl.ds(even, width + 8), :] += g
        return carry

    lax.fori_loop(0, pats.shape[0], visit, 0, unroll=True)


def visit_windows(offs, ext, probe, coeffs, pats, stacks):
    width = probe.shape[1]
    size = ext.shape[1]
    vmem = pl.BlockSpec(memory_space=pltpu.VMEM)
    return pl.pallas_call(
        visit_kernel,
        out_shape=(
            jax.ShapeDtypeStruct(ext.shape, jnp.float32),
            jax.ShapeDtypeStruct((6, width, width), jnp.float32),
        ),
        in_specs=[pl.BlockSpec(memory_space=pltpu.SMEM)] + [vmem] * 8,
        out_specs=(vmem, vmem),
        compiler_params=pltpu.CompilerParams(vmem_limit_bytes=40 * 1024 * 1024),
        name="visit_windows",
    )(offs, ext, probe, coeffs, pats, *stacks)


class Link:
    def __init__(self, axis, step, source, target, sems, slot):
        self.axis, self.step = axis, step
        here, count = lax.axis_index(axis), lax.axis_size(axis)
        self.copy = remote(
            source, target, sems, slot, {axis: lax.rem(here + step + count, count)}
        )

    def exists(self, step):
        here, count = lax.axis_index(self.axis), lax.axis_size(self.axis)
        return here > 0 if step < 0 else here < count - 1

    def start(self):
        pl.when(self.exists(self.step))(self.copy.start)
        return self

    def arrived(self, then=None):
        @pl.when(self.exists(-self.step))
        def _():
            self.copy.wait_recv()
            if then is not None:
                then()

    def sent(self):
        pl.when(self.exists(self.step))(self.copy.wait_send)


def remote(source, target, sems, slot, device):
    send, recv = sems
    where = tuple(device.get(axis, lax.axis_index(axis)) for axis in ("row", "col"))
    return pltpu.make_async_remote_copy(
        src_ref=source,
        dst_ref=target,
        send_sem=send.at[slot],
        recv_sem=recv.at[slot],
        device_id=where,
        device_id_type=pl.DeviceIdType.MESH,
    )


def greet():
    barrier = pltpu.get_barrier_semaphore()
    count = 0
    for axis in ("row", "col"):
        size = lax.axis_size(axis)
        here = lax.axis_index(axis)
        for distance in range(1, size):
            other = {"row": lax.axis_index("row"), "col": lax.axis_index("col")}
            other[axis] = lax.rem(here + distance, size)
            pl.semaphore_signal(
                barrier,
                inc=1,
                device_id=(other["row"], other["col"]),
                device_id_type=pl.DeviceIdType.MESH,
            )
            count += 1
    pl.semaphore_wait(barrier, count)


class Slots:
    def __init__(self, sems):
        self.sems, self.used = sems, 0

    def next(self):
        self.used += 1
        return self.used - 1


def copies_needed():
    rows, cols = lax.axis_size("row"), lax.axis_size("col")
    return 2 * (1 + cols + rows // 2) + cols + rows + 16


def halo_cols(field, part, half, tile, slots):
    inner = pl.ds(half, tile)
    return [
        Link("col", -1, field.at[part, inner, half : 2 * half],
             field.at[part, inner, half + tile :], slots.sems, slots.next()).start(),
        Link("col", 1, field.at[part, inner, tile : half + tile],
             field.at[part, inner, :half], slots.sems, slots.next()).start(),
    ]


def halo_rows(field, part, half, tile, slots):
    return [
        Link("row", -1, field.at[part, half : 2 * half, :],
             field.at[part, half + tile :, :], slots.sems, slots.next()).start(),
        Link("row", 1, field.at[part, tile : half + tile, :],
             field.at[part, :half, :], slots.sems, slots.next()).start(),
    ]


def fold_rows(grad, into, part, half, tile, slots):
    return [
        Link("row", -1, grad.at[part, :half, :], into.at[0, part], slots.sems, slots.next()).start(),
        Link("row", 1, grad.at[part, half + tile :, :], into.at[1, part], slots.sems, slots.next()).start(),
    ]


def fold_cols(mid, into, part, half, tile, slots):
    return [
        Link("col", -1, mid.at[part, :, :half], into.at[0, part], slots.sems, slots.next()).start(),
        Link("col", 1, mid.at[part, :, half + tile :], into.at[1, part], slots.sems, slots.next()).start(),
    ]


def update_kernel(last, grad, stats, field, coeffs, field_out, coeffs_out,
                  gfull, from_rows, mid, from_cols, half_sums, col_sums, shard, z_sums,
                  new_coeffs, sq_mine, sq_cols, sq_part, sq_rows, send_sem, recv_sem):
    rows, cols = lax.axis_size("row"), lax.axis_size("col")
    r, c = lax.axis_index("row"), lax.axis_index("col")
    depth = rows // 2
    k, z = lax.rem(r, 2), lax.div(r, 2)
    width = stats.shape[1]
    half = width // 2
    tile = grad.shape[1] - width
    slots = Slots((send_sem, recv_sem))
    rows1, rows2, rows3 = half_sums.shape[1], shard.shape[1], z_sums.shape[2]
    cut = rows3 < rows2

    gfull[...] = jnp.zeros_like(gfull)
    greet()

    def at(start, size):
        return pl.ds(pl.multiple_of(start, 8), size)

    def to(source, target, device):
        copy = remote(source, target, slots.sems, slots.next(), device)
        copy.start()
        return copy

    links = []

    def send(start, *refs):
        pair = start(*refs, half, tile, slots)
        links.extend(pair)
        return pair

    row_links = [send(fold_rows, grad, from_rows, part) for part in (0, 1)]
    partner = {"row": r + 1 - 2 * k}
    pair = to(stats.at[:, at((1 - k) * rows1, rows1), :], half_sums, partner)
    mid[...] = grad[:, half : half + tile, :]

    pair.wait_recv()
    half_sums[...] += stats[:, at(k * rows1, rows1), :]
    over_cols = []
    for d in range(1, cols):
        other = lax.rem(c + d, cols)
        over_cols.append(
            to(half_sums.at[:, at(other * rows2, rows2), :], col_sums.at[d - 1], {"col": other})
        )

    col_links = []
    for part in (0, 1):
        def add_low():
            mid[part, tile - half :, :] += from_rows[0, part]

        def add_high():
            mid[part, :half, :] += from_rows[1, part]

        row_links[part][0].arrived(add_low)
        row_links[part][1].arrived(add_high)
        col_links.append(send(fold_cols, mid, from_cols, part))

    for copy in over_cols:
        copy.wait_recv()
    shard[...] = half_sums[:, at(c * rows2, rows2), :] + sum(col_sums[d] for d in range(cols - 1))
    over_z = []
    for d in range(1, depth):
        other = lax.rem(z + d, depth)
        source = shard.at[:, at(other * rows3, rows3), :] if cut else shard
        over_z.append(to(source, z_sums.at[z], {"row": 2 * other + k}))
    z_sums[z] = shard[:, at(z * rows3, rows3), :] if cut else shard[...]

    inner = pl.ds(half, tile)
    side_links = []
    square = 0.0
    for part in (0, 1):
        gfull[part, inner, half : half + tile] = mid[part, :, half : half + tile]

        def add_low():
            gfull[part, inner, tile : half + tile] += from_cols[0, part]

        def add_high():
            gfull[part, inner, half : 2 * half] += from_cols[1, part]

        col_links[part][0].arrived(add_low)
        col_links[part][1].arrived(add_high)
        if not last:
            side_links.append(send(halo_cols, gfull, part))
        mine = gfull[part, inner, half : half + tile]
        square += jnp.sum((mine * mine).reshape(-1, 8, tile), axis=0)
    sq_mine[...] = sum(square[:, i : i + 128] for i in range(0, tile, 128))
    sq_over_cols = [
        to(sq_mine, sq_cols.at[d - 1], {"col": lax.rem(c + d, cols)}) for d in range(1, cols)
    ]

    for copy in over_z:
        copy.wait_recv()
    sums = sum(z_sums[i] for i in range(depth))
    base2 = k * rows1 + c * rows2
    base3 = base2 + z * rows3 if cut else base2
    new_coeffs[:, at(base3, rows3), :] = coeffs[:, at(base3, rows3), :] - sums[:3] / (sums[3:] + RIDGE)
    back = []
    if cut:
        ready = new_coeffs.at[:, at(base3, rows3), :]
        for d in range(1, depth):
            back.append(to(ready, ready, {"row": 2 * lax.rem(z + d, depth) + k}))

    for copy in sq_over_cols:
        copy.wait_recv()
    sq_part[...] = sq_mine[...] + sum(sq_cols[d] for d in range(cols - 1))
    sq_over_rows = [
        to(sq_part, sq_rows.at[d - 1], {"row": lax.rem(r + d, rows)}) for d in range(1, rows)
    ]

    end_links = []
    if not last:
        for part in (0, 1):
            for link in side_links[part]:
                link.arrived()
            end_links.append(send(halo_rows, gfull, part))
    for copy in back:
        copy.wait_recv()
    ready = new_coeffs.at[:, at(base2, rows2), :]
    wide = [to(ready, ready, {"col": lax.rem(c + d, cols)}) for d in range(1, cols)]

    for copy in sq_over_rows:
        copy.wait_recv()
    square = sq_part[...] + sum(sq_rows[d] for d in range(rows - 1))
    total = 2.0 * tile * tile * rows * cols
    rate = STEP_RATE / jnp.sqrt(jnp.sum(square, keepdims=True) / total + EPSILON)
    if last:
        for part in (0, 1):
            field_out[part] = field[part, inner, half : half + tile] - rate * gfull[part, inner, half : half + tile]

    for copy in wide:
        copy.wait_recv()
    ready = new_coeffs.at[:, at(k * rows1, rows1), :]
    final = to(ready, ready, partner)
    if not last:
        for part in (0, 1):
            for link in end_links[part]:
                link.arrived()
            field_out[part] = field[part] - rate * gfull[part]
    final.wait_recv()
    coeffs_out[...] = new_coeffs[...]
    for link in links:
        link.sent()
    for copy in [pair, final] + over_cols + sq_over_cols + sq_over_rows + over_z + back + wide:
        copy.wait_send()


def update(last, grad, stats, field, coeffs):
    rows, cols = lax.axis_size("row"), lax.axis_size("col")
    depth = rows // 2
    size, width = grad.shape[1], stats.shape[1]
    half, tile = width // 2, size - width
    rows1 = width // 2
    rows2 = rows1 // cols
    rows3 = rows2 // depth if rows2 % (8 * depth) == 0 else rows2
    vmem = pl.BlockSpec(memory_space=pltpu.VMEM)
    f32 = jnp.float32
    count = copies_needed()
    side = tile if last else size
    return pl.pallas_call(
        functools.partial(update_kernel, last),
        out_shape=(
            jax.ShapeDtypeStruct((2, side, side), f32),
            jax.ShapeDtypeStruct(coeffs.shape, f32),
        ),
        in_specs=[vmem] * 4,
        out_specs=(vmem, vmem),
        scratch_shapes=[
            pltpu.VMEM((2, size, size), f32),
            pltpu.VMEM((2, 2, half, size), f32),
            pltpu.VMEM((2, tile, size), f32),
            pltpu.VMEM((2, 2, tile, half), f32),
            pltpu.VMEM((6, rows1, width), f32),
            pltpu.VMEM((cols - 1, 6, rows2, width), f32),
            pltpu.VMEM((6, rows2, width), f32),
            pltpu.VMEM((depth, 6, rows3, width), f32),
            pltpu.VMEM(coeffs.shape, f32),
            pltpu.VMEM((8, 128), f32),
            pltpu.VMEM((cols - 1, 8, 128), f32),
            pltpu.VMEM((8, 128), f32),
            pltpu.VMEM((rows - 1, 8, 128), f32),
            pltpu.SemaphoreType.DMA((count,)),
            pltpu.SemaphoreType.DMA((count,)),
        ],
        compiler_params=pltpu.CompilerParams(
            collective_id=2 if last else 1,
            has_side_effects=True,
            vmem_limit_bytes=48 * 1024 * 1024,
        ),
        name="update_last" if last else "update",
    )(grad, stats, field, coeffs)


def extend_kernel(half, tile, field, out, full, send, recv):
    full[...] = jnp.zeros_like(full)
    inner = pl.ds(half, tile)
    full[:, inner, half : half + tile] = field[...]
    barrier = pltpu.get_barrier_semaphore()
    count = jnp.int32(0)
    for axis in ("row", "col"):
        size = lax.axis_size(axis)
        here = lax.axis_index(axis)
        for step in (-1, 1):
            other = {"row": lax.axis_index("row"), "col": lax.axis_index("col")}
            other[axis] = lax.rem(here + step + size, size)
            exists = here > 0 if step < 0 else here < size - 1
            count += exists.astype(jnp.int32)

            @pl.when(exists)
            def _():
                pl.semaphore_signal(
                    barrier,
                    inc=1,
                    device_id=(other["row"], other["col"]),
                    device_id_type=pl.DeviceIdType.MESH,
                )

    pl.semaphore_wait(barrier, count)
    slots = Slots((send, recv))
    side = [halo_cols(full, part, half, tile, slots) for part in (0, 1)]
    ends = []
    for part in (0, 1):
        for link in side[part]:
            link.arrived()
        ends.append(halo_rows(full, part, half, tile, slots))
    for part in (0, 1):
        for link in ends[part]:
            link.arrived()
    out[...] = full[...]
    for links in side + ends:
        for link in links:
            link.sent()


def extend(field, half):
    tile = field.shape[1]
    size = tile + 2 * half
    vmem = pl.BlockSpec(memory_space=pltpu.VMEM)
    return pl.pallas_call(
        functools.partial(extend_kernel, half, tile),
        out_shape=jax.ShapeDtypeStruct((2, size, size), jnp.float32),
        in_specs=[vmem],
        out_specs=vmem,
        scratch_shapes=[
            pltpu.VMEM((2, size, size), jnp.float32),
            pltpu.SemaphoreType.DMA((8,)),
            pltpu.SemaphoreType.DMA((8,)),
        ],
        compiler_params=pltpu.CompilerParams(
            collective_id=0, has_side_effects=True, vmem_limit_bytes=32 * 1024 * 1024
        ),
        name="extend",
    )(field)


def local(object_field, probe, coeffs, patterns, offsets):
    width = probe.shape[1]
    stacks = dft_stacks(width)
    flat_pats = patterns.reshape(-1, width, width)
    flat_offs = offsets.reshape(-1, 2)
    field = extend(object_field, width // 2)
    for turn in range(ITERS):
        grad, stats = visit_windows(flat_offs, field, probe, coeffs, flat_pats, stacks)
        field, coeffs = update(turn == ITERS - 1, grad, stats, field, coeffs)
    return (field, coeffs)


def solution(mesh):
    placed = (
        P(None, "row", "col"),
        P(),
        P(),
        P("row", "col", None, None, None),
        P("row", "col", None, None),
    )
    return jax.shard_map(
        local, mesh=mesh, in_specs=placed, out_specs=(P(None, "row", "col"), P()), check_vma=False
    )
```
